32 devices in a mesh: row: 8 (over y, x, core), col: 4 (over z).
Axes of the slice: x: 2, y: 2, z: 4, core: 2. Of those that a mesh axis runs over, the one named last changes fastest.
Arguments:
- forcing_terms: float32 [8, 4, 2, 32, 128], P('row', 'col'), may hold values from -6 to 6
- diagonal_reciprocal: float32 [8, 4, 2, 128, 128], P('row', 'col'), may hold values from -0.5 to 0.5
- stiffness_submatrix: float32 [8, 4, 32, 128, 128], P('row', 'col'), may hold values from -0.1875 to 0.1875
- stiffness_source_index: int32 [8, 4, 32], P('row', 'col'), may hold values from 0 to 7
- stiffness_target_index: int32 [8, 4, 32], P('row', 'col'), may hold values from 0 to 15
- stiffness_nonzero_tally: int32 [8, 4], P('row', 'col'), may hold values from 1 to 32, as said below
- interpolant_submatrix: float32 [8, 4, 16, 128, 128], P('row', 'col'), may hold values from -0.125 to 0.125
- interpolant_cluster_index: int32 [8, 4, 16], P('row', 'col'), may hold values from 0 to 1
- interpolant_target_index: int32 [8, 4, 16], P('row', 'col'), may hold values from 0 to 15
- interpolant_nonzero_tally: int32 [8, 4], P('row', 'col'), may hold values from 1 to 16, as said below
- provisional_interpolant: float32 [8, 4, 2, 128], P('row', 'col'), may hold values from 0.2 to 1
- cluster_label: int32 [8, 4, 2, 128], P('row', 'col'), may hold values from 0 to 255
Outputs:
- relaxed_iterate: float32 [8, 4, 2, 32, 128], P('row', 'col')
- residual: float32 [8, 4, 2, 32, 128], P('row', 'col')
- coarse: float32 [8, 2, 32, 128], P('row')
The draws below stay inside these ranges and needn't reach their ends.
Inputs may be any that keep to these rules, and one draw needn't show every extreme that they name: `stiffness_nonzero_tally`: tile slots at or past the count are unused; some pair has all 32 slots live in every draw. `interpolant_nonzero_tally`: tile slots at or past the count are unused; some pair has all 16 slots live in every draw.
All inputs are finite; a program needn't handle non-finite values.
Results may differ from the reference program's by a relative error of at most 0.0003.
Values sent between devices are 32-bit elements; how exact they have to be, the bound alone decides.
A program may use at most 64 MiB of HBM per device.

```python
import jax
import jax.numpy as jnp
from jax import lax

TILE_ORDER_SIZE = 128
PB = 2
RHS = 32
BAND_COUNT = 8
BAND_MEMBERS = 4
PAIR_CAPACITY = 32
PSLOT = 16


def skewed_counts(key, most):
    first_key = jax.random.fold_in(key, 5)
    second_key = jax.random.fold_in(key, 9)
    base = jax.random.randint(first_key, (BAND_COUNT * BAND_MEMBERS,), 1, most + 1)
    chosen = jax.random.randint(second_key, (), 0, BAND_COUNT * BAND_MEMBERS)
    filled = jnp.where(jnp.arange(BAND_COUNT * BAND_MEMBERS) == chosen, most, base)
    return filled.reshape(BAND_COUNT, BAND_MEMBERS).astype(jnp.int32)


def draw_stiffness_nonzero_tally(key, part):
    return skewed_counts(jax.random.fold_in(key, 11), PAIR_CAPACITY)


def draw_interpolant_nonzero_tally(key, part):
    return skewed_counts(jax.random.fold_in(key, 23), PSLOT)


def place_ends(drawn, rng, low, high):
    extent = drawn.shape
    index_at = [jax.random.randint(jax.random.fold_in(rng, axis), (), 0, extent[axis]) for axis in range(len(extent))]
    drawn = drawn.at[tuple(index_at)].set(low)
    longest = extent.index(max(extent))
    index_at[longest] = (index_at[longest] + 1) % extent[longest]
    return drawn.at[tuple(index_at)].set(high)


def shard_levels(rng, dims, shards, least, high):
    loudness, own = 1.0, jax.random.fold_in(rng, 6)
    for position, shards_of in shards:
        steps = jnp.exp(jax.random.uniform(jax.random.fold_in(own, position), (shards_of,), jnp.float32, least / len(shards), high / len(shards)))
        loudness = loudness * jnp.repeat(steps, dims[position] // shards_of).reshape([-1 if axis == position else 1 for axis in range(len(dims))])
    return loudness


def centred(stream_key, shape, width, limit, split=(), held_as=jnp.bfloat16):
    drawn = width * jax.random.normal(stream_key, shape, jnp.float32)
    if split:
        drawn = drawn * shard_levels(stream_key, shape, split, -0.22, 0.18)
    return jnp.clip(drawn, -limit, limit).astype(held_as)


def setup_inputs(seed: int = 0) -> dict:
    keys = jax.random.split(jax.random.key(seed), 13)
    return {
        "forcing_terms": centred(keys[0], (BAND_COUNT, BAND_MEMBERS, PB, RHS, TILE_ORDER_SIZE), 1.0, 6.0, ((0, 8), (1, 4)), jnp.float32),
        "diagonal_reciprocal": centred(keys[1], (BAND_COUNT, BAND_MEMBERS, PB, TILE_ORDER_SIZE, TILE_ORDER_SIZE), TILE_ORDER_SIZE ** -0.5, 0.5, ((0, 8), (1, 4)), jnp.float32),
        "stiffness_submatrix": centred(keys[2], (BAND_COUNT, BAND_MEMBERS, PAIR_CAPACITY, TILE_ORDER_SIZE, TILE_ORDER_SIZE), (TILE_ORDER_SIZE * 8) ** -0.5, 0.1875, ((0, 8), (1, 4)), jnp.float32),
        "stiffness_source_index": place_ends(jax.random.randint(keys[3], (BAND_COUNT, BAND_MEMBERS, PAIR_CAPACITY), 0, BAND_MEMBERS * PB), jax.random.fold_in(keys[3], 1), 0, (BAND_MEMBERS * PB) - 1).astype(jnp.int32),
        "stiffness_target_index": place_ends(jax.random.randint(keys[4], (BAND_COUNT, BAND_MEMBERS, PAIR_CAPACITY), 0, BAND_COUNT * PB), jax.random.fold_in(keys[4], 1), 0, (BAND_COUNT * PB) - 1).astype(jnp.int32),
        "stiffness_nonzero_tally": draw_stiffness_nonzero_tally(jax.random.fold_in(keys[12], 71), 0),
        "interpolant_submatrix": centred(keys[6], (BAND_COUNT, BAND_MEMBERS, PSLOT, TILE_ORDER_SIZE, TILE_ORDER_SIZE), (TILE_ORDER_SIZE * 4 * BAND_MEMBERS) ** -0.5, 0.125, ((0, 8), (1, 4)), jnp.float32),
        "interpolant_cluster_index": place_ends(jax.random.randint(keys[7], (BAND_COUNT, BAND_MEMBERS, PSLOT), 0, PB), jax.random.fold_in(keys[7], 1), 0, PB - 1).astype(jnp.int32),
        "interpolant_target_index": place_ends(jax.random.randint(keys[8], (BAND_COUNT, BAND_MEMBERS, PSLOT), 0, BAND_COUNT * PB), jax.random.fold_in(keys[8], 1), 0, (BAND_COUNT * PB) - 1).astype(jnp.int32),
        "interpolant_nonzero_tally": draw_interpolant_nonzero_tally(jax.random.fold_in(keys[12], 71), 0),
        "provisional_interpolant": jnp.clip(0.2 + 0.8 * jax.random.uniform(keys[10], (BAND_COUNT, BAND_MEMBERS, PB, TILE_ORDER_SIZE), jnp.float32) ** shard_levels(keys[10], (BAND_COUNT, BAND_MEMBERS, PB, TILE_ORDER_SIZE), ((0, 8), (1, 4)), -0.2, 0.2), 0.2, 1.0),
        "cluster_label": place_ends(jax.random.randint(keys[11], (BAND_COUNT, BAND_MEMBERS, PB, TILE_ORDER_SIZE), 0, PB * TILE_ORDER_SIZE), jax.random.fold_in(keys[11], 1), 0, (PB * TILE_ORDER_SIZE) - 1).astype(jnp.int32),
    }


omega = 0.7
highest = lax.Precision.HIGHEST


def tile_terms(blocks, stiffness_submatrices, rows, cols, count, nout):
    inputs = jnp.take(blocks, cols, axis=0)
    product = jnp.einsum('ska,sab->skb', inputs, stiffness_submatrices, precision=highest)
    live = (jnp.arange(stiffness_submatrices.shape[0]) < count).astype(jnp.float32)
    onehot = (rows[:, None] == jnp.arange(nout)[None, :]).astype(jnp.float32) * live[:, None]
    return jnp.einsum('so,skb->okb', onehot, product, precision=highest)


def precondition(vec, diagonal_reciprocal):
    return jnp.einsum('ijpka,ijpab->ijpkb', vec, diagonal_reciprocal, precision=highest)


def stiffness_product(vec, stiffness_submatrices, rows, cols, counts):
    nrg, ncg, pb, nrhs, blk = vec.shape

    def one_row(args):
        tile_row, row_ids, col_ids, count_row = args

        def one_col(index, tiles_one, rows_one, cols_one, count_one):
            blocks = jnp.take(vec, index, axis=1).reshape(nrg * pb, nrhs, blk)
            return tile_terms(blocks, tiles_one, rows_one, cols_one, count_one, ncg * pb)

        terms = jax.vmap(one_col)(jnp.arange(ncg), tile_row, row_ids, col_ids, count_row)
        return jnp.sum(terms, axis=0).reshape(ncg, pb, nrhs, blk)

    return lax.map(one_row, (stiffness_submatrices, rows, cols, counts))


def restrict(residual, interpolant_submatrix, interpolant_cluster_index, interpolant_target_index, interpolant_nonzero_tally, provisional_interpolant, cluster_label):
    nrg, ncg, pb, nrhs, blk = residual.shape

    def one_row(args):
        tile_row, row_ids, col_ids, count_row, tent_row, agg_row, resid_row = args

        def one_col(index, tiles_one, rows_one, cols_one, count_one, tent_one, agg_one, resid_one):
            blocks = jnp.take(residual, index, axis=1).reshape(nrg * pb, nrhs, blk)
            part = tile_terms(blocks, tiles_one, rows_one, cols_one, count_one, pb)
            weighted = (resid_one * tent_one[:, None, :]).transpose(1, 0, 2).reshape(nrhs, pb * blk)
            onehot = (agg_one.reshape(-1)[:, None] == jnp.arange(pb * blk)[None, :]).astype(jnp.float32)
            tentative = jnp.dot(weighted, onehot, precision=highest)
            return part + tentative.reshape(nrhs, pb, blk).transpose(1, 0, 2)

        terms = jax.vmap(one_col)(jnp.arange(ncg), tile_row, row_ids, col_ids, count_row, tent_row, agg_row, resid_row)
        return jnp.sum(terms, axis=0)

    return lax.map(one_row, (interpolant_submatrix, interpolant_cluster_index, interpolant_target_index, interpolant_nonzero_tally, provisional_interpolant, cluster_label, residual))


def reference(forcing_terms, diagonal_reciprocal, stiffness_submatrix, stiffness_source_index, stiffness_target_index, stiffness_nonzero_tally, interpolant_submatrix, interpolant_cluster_index, interpolant_target_index, interpolant_nonzero_tally, provisional_interpolant, cluster_label):
    starting_guess = omega * precondition(forcing_terms, diagonal_reciprocal)
    image_field = stiffness_product(starting_guess, stiffness_submatrix, stiffness_source_index, stiffness_target_index, stiffness_nonzero_tally)
    relaxed_iterate = starting_guess + omega * precondition(forcing_terms - image_field, diagonal_reciprocal)
    image_field = stiffness_product(relaxed_iterate, stiffness_submatrix, stiffness_source_index, stiffness_target_index, stiffness_nonzero_tally)
    residual = forcing_terms - image_field
    coarse = restrict(residual, interpolant_submatrix, interpolant_cluster_index, interpolant_target_index, interpolant_nonzero_tally, provisional_interpolant, cluster_label)
    return relaxed_iterate, residual, coarse
```

```python
import functools

import jax
import jax.numpy as jnp
from jax import lax
from jax.experimental import pallas as pl
from jax.experimental.pallas import tpu as pltpu
from jax.sharding import PartitionSpec as P

omega = 0.7
MESH = pl.DeviceIdType.MESH
f32, bf16 = jnp.float32, jnp.bfloat16
unrolled_most = 8
slot_group = 8


def loop(low, high, step):
    if high - low <= unrolled_most:
        for index in range(low, high):
            step(index)
    else:

        def one(index, carry):
            step(index)
            return carry

        lax.fori_loop(low, high, one, 0)


def split(value):
    high = value.astype(bf16)
    low = (value - high.astype(f32)).astype(bf16)
    return high, low


def wide(value):
    return jnp.concatenate(split(value), axis=-1)


def times(left, weight):
    both = jnp.dot(left, weight, preferred_element_type=f32)
    half = both.shape[-1] // 2
    return both[:, :half] + both[:, half:]


def kernel(
    nr, nc,
    f_hbm, d_hbm, a_hbm, src_s, tgt_s, cnt_s, b_hbm, clu_s, btgt_s, bcnt_s, w_ref, lab_ref,
    x_out, r_out, c_out,
    f_v, d_v, a_v, b_v, wd, wa, wb, gath, xs, prod, part, pieces, coarse_v, onehot,
    x_v, c_v, live_a, live_b,
    in_sem, a_sem, out_sem, rsend, rrecv, csend, crecv,
):
    pb, nrhs, blk = f_v.shape
    slots, bslots = a_v.shape[0], b_v.shape[0]
    chunks = a_sem.shape[0]
    per = slots // chunks
    row, col = lax.axis_index("row"), lax.axis_index("col")

    f_in = pltpu.make_async_copy(f_hbm.at[0, 0], f_v, in_sem.at[0])
    d_in = pltpu.make_async_copy(d_hbm.at[0, 0], d_v, in_sem.at[1])
    b_in = pltpu.make_async_copy(b_hbm.at[0, 0], b_v, in_sem.at[2])
    a_in = [
        pltpu.make_async_copy(a_hbm.at[0, 0, pl.ds(c * per, per)], a_v.at[pl.ds(c * per, per)], a_sem.at[c])
        for c in range(chunks)
    ]
    d_in.start()
    f_in.start()
    for copy in a_in:
        copy.start()
    b_in.start()

    barrier = pltpu.get_barrier_semaphore()

    def greet_row(k):
        pl.semaphore_signal(barrier, inc=1, device_id={"row": lax.rem(row + k, nr)}, device_id_type=MESH)

    def greet_col(k):
        pl.semaphore_signal(barrier, inc=1, device_id={"col": lax.rem(col + k, nc)}, device_id_type=MESH)

    loop(1, nr, greet_row)
    loop(1, nc, greet_col)

    def row_copy(phase, k, owner):
        return pltpu.make_async_remote_copy(
            src_ref=gath.at[phase, owner],
            dst_ref=gath.at[phase, owner],
            send_sem=rsend.at[phase, k],
            recv_sem=rrecv.at[phase, k],
            device_id={"row": lax.rem(row + k, nr)},
            device_id_type=MESH,
        )

    def spread(phase):
        loop(1, nr, lambda k: row_copy(phase, k, row).start())

    def collect(phase):
        def take(owner):
            for p in range(pb):
                xs[owner * pb + p] = wide(gath[phase, owner, p])

        take(row)

        def arrive(k):
            owner = lax.rem(row + nr - k, nr)
            row_copy(phase, k, owner).wait_recv()
            take(owner)

        loop(1, nr, arrive)

    def piece_copy(phase, k, owner, source):
        return pltpu.make_async_remote_copy(
            src_ref=part.at[phase, owner],
            dst_ref=pieces.at[phase, source],
            send_sem=csend.at[phase, k],
            recv_sem=crecv.at[phase, k],
            device_id={"col": lax.rem(col + k, nc)},
            device_id_type=MESH,
        )

    def prepare(weight, k, tile):
        both = wide(tile)
        weight[k, :blk] = both
        weight[k, blk:] = both

    def products(weight, target, count):
        def group(index, carry):
            for j in range(slot_group):
                s = index * slot_group + j
                prod[s] = times(xs[target[0, 0, s]], weight[s])
            return carry

        lax.fori_loop(0, count // slot_group, group, 0)

    def chosen(live, count, block):
        total = jnp.zeros((nrhs, blk), f32)
        for s in range(count):
            total = total + jnp.where(live[s] == block, prod[s], 0.0)
        return total

    def operator(phase):
        collect(phase)
        products(wa, tgt_s, slots)

        def piece(k):
            owner = lax.rem(col + k, nc)
            for p in range(pb):
                part[phase, owner, p] = chosen(live_a, slots, owner * pb + p)
            piece_copy(phase, k, owner, col).start()

        loop(1, nc, piece)
        image = [chosen(live_a, slots, col * pb + p) for p in range(pb)]
        for p in range(pb):
            pieces[phase, col, p] = image[p]

        def arrive(k):
            source = lax.rem(col + nc - k, nc)
            piece_copy(phase, k, col, source).wait_recv()

        loop(1, nc, arrive)
        return [jnp.sum(pieces[phase, :, p], axis=0) for p in range(pb)]

    d_in.wait()
    for p in range(pb):
        prepare(wd, p, d_v[p])
    f_in.wait()
    for p in range(pb):
        gath[0, row, p] = omega * times(wide(f_v[p]), wd[p])
    pl.semaphore_wait(barrier, nr + nc - 2)
    spread(0)

    for c in range(chunks):
        a_in[c].wait()

        def prepare_a(j, carry):
            prepare(wa, c * per + j, a_v[c * per + j])
            return carry

        lax.fori_loop(0, per, prepare_a, 0)

    def keep_a(s, carry):
        live_a[s] = jnp.where(s < cnt_s[0, 0], src_s[0, 0, s], -1)
        return carry

    lax.fori_loop(0, slots, keep_a, 0)

    image = operator(0)
    for p in range(pb):
        x = gath[0, row, p] + omega * times(wide(f_v[p] - image[p]), wd[p])
        gath[1, row, p] = x
        x_v[p] = x
    spread(1)
    x_copy = pltpu.make_async_copy(x_v, x_out.at[0, 0], out_sem.at[0])
    x_copy.start()

    b_in.wait()

    def prepare_b(j, carry):
        prepare(wb, j, b_v[j])
        return carry

    lax.fori_loop(0, bslots, prepare_b, 0)

    def keep_b(s, carry):
        live_b[s] = jnp.where(s < bcnt_s[0, 0], clu_s[0, 0, s], -1)
        return carry

    lax.fori_loop(0, bslots, keep_b, 0)
    aggregate = lax.broadcasted_iota(jnp.int32, (pb * blk, blk), 0)
    for p in range(pb):
        same = aggregate == lab_ref[0, 0, p : p + 1, :]
        onehot[:, p * blk : (p + 1) * blk] = jnp.where(same, 1.0, 0.0).astype(bf16)

    image = operator(1)
    for p in range(pb):
        gath[2, row, p] = f_v[p] - image[p]
    spread(2)
    r_copy = pltpu.make_async_copy(gath.at[2, row], r_out.at[0, 0], out_sem.at[1])
    r_copy.start()

    weighted = jnp.concatenate(
        [gath[2, row, p] * w_ref[0, 0, p : p + 1, :] for p in range(pb)], axis=-1
    )
    contract = functools.partial(
        lax.dot_general,
        dimension_numbers=(((1,), (1,)), ((), ())),
        preferred_element_type=f32,
    )
    high, low = split(weighted)
    tentative = contract(high, onehot[...]) + contract(low, onehot[...])
    for p in range(pb):
        c_v[p] = tentative[:, p * blk : (p + 1) * blk]

    collect(2)
    products(wb, btgt_s, bslots)
    for p in range(pb):
        coarse_v[col, p] = c_v[p] + chosen(live_b, bslots, p)

    def coarse_copy(k, source):
        return pltpu.make_async_remote_copy(
            src_ref=coarse_v.at[source],
            dst_ref=coarse_v.at[source],
            send_sem=csend.at[2, k],
            recv_sem=crecv.at[2, k],
            device_id={"col": lax.rem(col + k, nc)},
            device_id_type=MESH,
        )

    loop(1, nc, lambda k: coarse_copy(k, col).start())
    loop(1, nc, lambda k: coarse_copy(k, lax.rem(col + nc - k, nc)).wait_recv())
    for p in range(pb):
        c_v[p] = jnp.sum(coarse_v[:, p], axis=0)
    c_copy = pltpu.make_async_copy(c_v, c_out.at[0], out_sem.at[2])
    c_copy.start()

    for phase in range(3):
        loop(1, nr, lambda k: row_copy(phase, k, row).wait_send())
    for phase in range(2):
        loop(1, nc, lambda k: piece_copy(phase, k, lax.rem(col + k, nc), col).wait_send())
    loop(1, nc, lambda k: coarse_copy(k, col).wait_send())
    x_copy.wait()
    r_copy.wait()
    c_copy.wait()


def body(nr, nc, *args):
    f, d, a, src, tgt, cnt, b, clu, btgt, bcnt, w, lab = args
    pb, nrhs, blk = f.shape[2:]
    slots, bslots = a.shape[2], b.shape[2]
    chunks = 4
    anyspace = pl.BlockSpec(memory_space=pl.ANY)
    smem = pl.BlockSpec(memory_space=pltpu.SMEM)
    vmem = pl.BlockSpec(memory_space=pltpu.VMEM)
    block = (pb, nrhs, blk)
    dma = pltpu.SemaphoreType.DMA
    flops = 8 * (2 * slots + bslots + 3 * pb) * nrhs * blk * blk
    return pl.pallas_call(
        functools.partial(kernel, nr, nc),
        out_shape=(
            jax.ShapeDtypeStruct(f.shape, f32),
            jax.ShapeDtypeStruct(f.shape, f32),
            jax.ShapeDtypeStruct((1,) + block, f32),
        ),
        in_specs=[anyspace, anyspace, anyspace, smem, smem, smem, anyspace, smem, smem, smem, vmem, vmem],
        out_specs=(anyspace, anyspace, anyspace),
        scratch_shapes=[
            pltpu.VMEM(block, f32),
            pltpu.VMEM((pb, blk, blk), f32),
            pltpu.VMEM((slots, blk, blk), f32),
            pltpu.VMEM((bslots, blk, blk), f32),
            pltpu.VMEM((pb, 2 * blk, 2 * blk), bf16),
            pltpu.VMEM((slots, 2 * blk, 2 * blk), bf16),
            pltpu.VMEM((bslots, 2 * blk, 2 * blk), bf16),
            pltpu.VMEM((3, nr) + block, f32),
            pltpu.VMEM((nr * pb, nrhs, 2 * blk), bf16),
            pltpu.VMEM((slots, nrhs, blk), f32),
            pltpu.VMEM((2, nc) + block, f32),
            pltpu.VMEM((2, nc) + block, f32),
            pltpu.VMEM((nc,) + block, f32),
            pltpu.VMEM((pb * blk, pb * blk), bf16),
            pltpu.VMEM(block, f32),
            pltpu.VMEM(block, f32),
            pltpu.SMEM((slots,), jnp.int32),
            pltpu.SMEM((bslots,), jnp.int32),
            dma((3,)),
            dma((chunks,)),
            dma((3,)),
            dma((3, nr)),
            dma((3, nr)),
            dma((3, nc)),
            dma((3, nc)),
        ],
        compiler_params=pltpu.CompilerParams(
            collective_id=0, has_side_effects=True, vmem_limit_bytes=40 * 1024 * 1024
        ),
        cost_estimate=pl.CostEstimate(
            flops=flops, bytes_accessed=4 * blk * blk * (slots + bslots + pb), transcendentals=0
        ),
    )(f, d, a, src, tgt, cnt, b, clu, btgt, bcnt, w, lab)


def solution(mesh):
    tensor = P("row", "col", None, None, None)
    index = P("row", "col", None)
    plain = P("row", "col", None, None)
    tally = P("row", "col")
    return jax.shard_map(
        functools.partial(body, mesh.shape["row"], mesh.shape["col"]),
        mesh=mesh,
        in_specs=(tensor, tensor, tensor, index, index, tally, tensor, index, index, tally, plain, plain),
        out_specs=(tensor, tensor, P("row", None, None, None)),
        check_vma=False,
    )
```

```python
import functools

import jax
import jax.numpy as jnp
from jax import lax
from jax.experimental import pallas as pl
from jax.experimental.pallas import tpu as pltpu
from jax.sharding import PartitionSpec as P

omega = 0.7
MESH = pl.DeviceIdType.MESH
f32, bf16 = jnp.float32, jnp.bfloat16
unrolled_most = 8
slot_group = 8
vmem_bytes = 60 * 1024 * 1024
halves = 2


def loop(low, high, step):
    if high - low <= unrolled_most:
        for index in range(low, high):
            step(index)
    else:

        def one(index, carry):
            step(index)
            return carry

        lax.fori_loop(low, high, one, 0)


def split(value):
    high = value.astype(bf16)
    low = (value - high.astype(f32)).astype(bf16)
    return high, low


def wide(value):
    return jnp.concatenate(split(value), axis=-1)


def times(left, weight):
    both = jnp.dot(left, weight, preferred_element_type=f32)
    half = both.shape[-1] // 2
    return both[:, :half] + both[:, half:]


def kernel(
    nr, nc, parts,
    f_hbm, d_hbm, a_hbm, src_h, tgt_h, cnt_s, b_hbm, clu_h, btgt_h, bcnt_s, w_h, lab_h,
    x_out, r_out, c_out,
    f_v, d_v, a_v, b_v, wd, wa, wb, gath, xs, prod, part, pieces, coarse_v, onehot,
    x_v, r_v, c_v, live_a, live_b, src_s, tgt_s, clu_s, btgt_s, w_ref, lab_ref,
    in_sem, small_sem, a_sem, out_sem, rsend, rrecv, csend, crecv,
):
    pb, nrhs, blk = f_v.shape
    some = nrhs // parts
    slots, bslots = a_v.shape[0], b_v.shape[0]
    chunks = a_sem.shape[0]
    per = slots // chunks
    row, col = lax.axis_index("row"), lax.axis_index("col")

    d_in = pltpu.make_async_copy(d_hbm.at[0, 0], d_v, in_sem.at[0])
    f_in = pltpu.make_async_copy(f_hbm.at[0, 0], f_v, in_sem.at[1])
    b_in = pltpu.make_async_copy(b_hbm.at[0, 0], b_v, in_sem.at[2])
    a_in = [
        pltpu.make_async_copy(a_hbm.at[0, 0, pl.ds(c * per, per)], a_v.at[pl.ds(c * per, per)], a_sem.at[c])
        for c in range(chunks)
    ]
    small = [
        pltpu.make_async_copy(source, held, small_sem.at[i])
        for i, (source, held) in enumerate(
            ((tgt_h, tgt_s), (src_h, src_s), (btgt_h, btgt_s), (clu_h, clu_s), (w_h, w_ref), (lab_h, lab_ref))
        )
    ]
    d_in.start()
    f_in.start()

    barrier = pltpu.get_barrier_semaphore()

    def greet_row(k):
        pl.semaphore_signal(barrier, inc=1, device_id={"row": lax.rem(row + k, nr)}, device_id_type=MESH)

    def greet_col(k):
        pl.semaphore_signal(barrier, inc=1, device_id={"col": lax.rem(col + k, nc)}, device_id_type=MESH)

    loop(1, nr, greet_row)
    loop(1, nc, greet_col)
    for copy in a_in:
        copy.start()
    for copy in small:
        copy.start()
    b_in.start()

    def rows_of(h):
        return slice(h * some, (h + 1) * some)

    def row_copy(phase, h, k, owner):
        return pltpu.make_async_remote_copy(
            src_ref=gath.at[phase, h, owner],
            dst_ref=gath.at[phase, h, owner],
            send_sem=rsend.at[phase, h, k],
            recv_sem=rrecv.at[phase, h, k],
            device_id={"row": lax.rem(row + k, nr)},
            device_id_type=MESH,
        )

    def spread(phase, h):
        loop(1, nr, lambda k: row_copy(phase, h, k, row).start())

    def collect(phase, h):
        def take(owner):
            for p in range(pb):
                xs[owner * pb + p] = wide(gath[phase, h, owner, p])

        take(row)

        def arrive(k):
            owner = lax.rem(row + nr - k, nr)
            row_copy(phase, h, k, owner).wait_recv()
            take(owner)

        loop(1, nr, arrive)

    def piece_copy(phase, h, k, owner, source):
        return pltpu.make_async_remote_copy(
            src_ref=part.at[phase, h, owner],
            dst_ref=pieces.at[phase, h, source],
            send_sem=csend.at[phase, h, k],
            recv_sem=crecv.at[phase, h, k],
            device_id={"col": lax.rem(col + k, nc)},
            device_id_type=MESH,
        )

    def coarse_copy(h, k, source):
        return pltpu.make_async_remote_copy(
            src_ref=coarse_v.at[h, source],
            dst_ref=coarse_v.at[h, source],
            send_sem=csend.at[2, h, k],
            recv_sem=crecv.at[2, h, k],
            device_id={"col": lax.rem(col + k, nc)},
            device_id_type=MESH,
        )

    def source_of(k):
        return lax.rem(col + nc - k, nc)

    def prepare(weight, k, tile):
        both = wide(tile)
        weight[k, :blk] = both
        weight[k, blk:] = both

    def products(weight, target, count):
        def group(index, carry):
            for j in range(slot_group):
                s = index * slot_group + j
                prod[s] = times(xs[target[0, 0, s]], weight[s])
            return carry

        lax.fori_loop(0, count // slot_group, group, 0)

    def chosen(live, count, first):
        totals = [jnp.zeros((some, blk), f32) for p in range(pb)]
        for s in range(count):
            held, block = prod[s], live[s] - first
            totals = [total + jnp.where(block == p, held, 0.0) for p, total in enumerate(totals)]
        return totals

    def forward(phase, h):
        collect(phase, h)
        products(wa, tgt_s, slots)

        def piece(k, carry):
            owner = lax.rem(col + k, nc)
            for p, total in enumerate(chosen(live_a, slots, owner * pb)):
                part[phase, h, owner, p] = total

            @pl.when(k < nc)
            def _():
                piece_copy(phase, h, k, owner, col).start()

            return carry

        lax.fori_loop(1, nc + 1, piece, 0)

    def both(step):
        def one(h, carry):
            step(h)
            return carry

        lax.fori_loop(0, parts, one, 0)

    def image(phase, h):
        loop(1, nc, lambda k: piece_copy(phase, h, k, col, source_of(k)).wait_recv())
        totals = [part[phase, h, col, p] for p in range(pb)]
        for k in range(1, nc):
            totals = [total + pieces[phase, h, source_of(k), p] for p, total in enumerate(totals)]
        return totals

    d_in.wait()
    for p in range(pb):
        prepare(wd, p, d_v[p])
    f_in.wait()
    for p in range(pb):
        x = omega * times(wide(f_v[p]), wd[p])
        for h in range(parts):
            gath[0, h, row, p] = x[rows_of(h)]
    pl.semaphore_wait(barrier, nr + nc - 2)
    for h in range(parts):
        spread(0, h)

    for c in range(chunks):
        a_in[c].wait()

        def prepare_a(j, carry):
            prepare(wa, c * per + 2 * j, a_v[c * per + 2 * j])
            prepare(wa, c * per + 2 * j + 1, a_v[c * per + 2 * j + 1])
            return carry

        lax.fori_loop(0, per // 2, prepare_a, 0)

    for copy in small:
        copy.wait()

    def keep_a(s, carry):
        live_a[s] = jnp.where(s < cnt_s[0, 0], src_s[0, 0, s], -1)
        return carry

    lax.fori_loop(0, slots, keep_a, 0)

    both(lambda h: forward(0, h))

    b_in.wait()

    def prepare_b(j, carry):
        prepare(wb, j, b_v[j])
        return carry

    def keep_b(s, carry):
        live_b[s] = jnp.where(s < bcnt_s[0, 0], clu_s[0, 0, s], -1)
        return carry

    for h in range(parts):
        total = image(0, h)
        for p in range(pb):
            right = f_v[p, rows_of(h)] - total[p]
            x = gath[0, h, row, p] + omega * times(wide(right), wd[p])
            gath[1, h, row, p] = x
            x_v[p, rows_of(h)] = x
        spread(1, h)
    x_copy = pltpu.make_async_copy(x_v, x_out.at[0, 0], out_sem.at[0])
    x_copy.start()

    lax.fori_loop(0, bslots, prepare_b, 0)
    lax.fori_loop(0, bslots, keep_b, 0)
    aggregate = lax.broadcasted_iota(jnp.int32, (pb * blk, blk), 0)
    for p in range(pb):
        same = aggregate == lab_ref[0, 0, p : p + 1, :]
        onehot[:, p * blk : (p + 1) * blk] = jnp.where(same, 1.0, 0.0).astype(bf16)

    both(lambda h: forward(1, h))
    for h in range(parts):
        total = image(1, h)
        for p in range(pb):
            left = f_v[p, rows_of(h)] - total[p]
            gath[2, h, row, p] = left
            r_v[p, rows_of(h)] = left
        spread(2, h)
    r_copy = pltpu.make_async_copy(r_v, r_out.at[0, 0], out_sem.at[1])
    r_copy.start()

    weighted = jnp.concatenate([r_v[p] * w_ref[0, 0, p : p + 1, :] for p in range(pb)], axis=-1)
    contract = functools.partial(
        lax.dot_general,
        dimension_numbers=(((1,), (1,)), ((), ())),
        preferred_element_type=f32,
    )
    high, low = split(weighted)
    tentative = contract(high, onehot[...]) + contract(low, onehot[...])
    for p in range(pb):
        for h in range(parts):
            coarse_v[h, col, p] = tentative[rows_of(h), p * blk : (p + 1) * blk]

    def restrict(h):
        collect(2, h)
        products(wb, btgt_s, bslots)
        for p, total in enumerate(chosen(live_b, bslots, 0)):
            coarse_v[h, col, p] = coarse_v[h, col, p] + total
        loop(1, nc, lambda k: coarse_copy(h, k, col).start())

    both(restrict)

    for phase in range(3):
        for h in range(parts):
            loop(1, nr, lambda k: row_copy(phase, h, k, row).wait_send())
    for phase in range(2):
        for h in range(parts):
            loop(1, nc, lambda k: piece_copy(phase, h, k, lax.rem(col + k, nc), col).wait_send())
    x_copy.wait()
    r_copy.wait()
    for h in range(parts):
        loop(1, nc, lambda k: coarse_copy(h, k, source_of(k)).wait_recv())
        for p in range(pb):
            c_v[p, rows_of(h)] = jnp.sum(coarse_v[h, :, p], axis=0)
    c_copy = pltpu.make_async_copy(c_v, c_out.at[0], out_sem.at[2])
    c_copy.start()
    for h in range(parts):
        loop(1, nc, lambda k: coarse_copy(h, k, col).wait_send())
    c_copy.wait()


def body(nr, nc, *args):
    f, d, a, src, tgt, cnt, b, clu, btgt, bcnt, w, lab = args
    pb, nrhs, blk = f.shape[2:]
    slots, bslots = a.shape[2], b.shape[2]
    chunks = 4
    parts = halves
    some = (pb, nrhs // parts, blk)
    anyspace = pl.BlockSpec(memory_space=pl.ANY)
    smem = pl.BlockSpec(memory_space=pltpu.SMEM)
    block = (pb, nrhs, blk)
    dma = pltpu.SemaphoreType.DMA
    flops = 8 * (2 * slots + bslots + 3 * pb) * nrhs * blk * blk
    shapes = (
        jax.ShapeDtypeStruct(f.shape, f32),
        jax.ShapeDtypeStruct(f.shape, f32),
        jax.ShapeDtypeStruct((1,) + block, f32),
    )
    return pl.pallas_call(
        functools.partial(kernel, nr, nc, parts),
        out_shape=tuple(pltpu.VMEM(x.shape, x.dtype) for x in shapes),
        in_specs=[anyspace] * 5 + [smem] + [anyspace] * 3 + [smem] + [anyspace] * 2,
        out_specs=(anyspace,) * 3,
        scratch_shapes=[
            pltpu.VMEM(block, f32),
            pltpu.VMEM((pb, blk, blk), f32),
            pltpu.VMEM((slots, blk, blk), f32),
            pltpu.VMEM((bslots, blk, blk), f32),
            pltpu.VMEM((pb, 2 * blk, 2 * blk), bf16),
            pltpu.VMEM((slots, 2 * blk, 2 * blk), bf16),
            pltpu.VMEM((bslots, 2 * blk, 2 * blk), bf16),
            pltpu.VMEM((3, parts, nr) + some, f32),
            pltpu.VMEM((nr * pb, some[1], 2 * blk), bf16),
            pltpu.VMEM((slots, some[1], blk), f32),
            pltpu.VMEM((2, parts, nc) + some, f32),
            pltpu.VMEM((2, parts, nc) + some, f32),
            pltpu.VMEM((parts, nc) + some, f32),
            pltpu.VMEM((pb * blk, pb * blk), bf16),
            pltpu.VMEM(block, f32),
            pltpu.VMEM(block, f32),
            pltpu.VMEM(block, f32),
            pltpu.SMEM((slots,), jnp.int32),
            pltpu.SMEM((bslots,), jnp.int32),
            pltpu.SMEM(src.shape, jnp.int32),
            pltpu.SMEM(tgt.shape, jnp.int32),
            pltpu.SMEM(clu.shape, jnp.int32),
            pltpu.SMEM(btgt.shape, jnp.int32),
            pltpu.VMEM(w.shape, f32),
            pltpu.VMEM(lab.shape, jnp.int32),
            dma((3,)),
            dma((6,)),
            dma((chunks,)),
            dma((3,)),
            dma((3, parts, nr)),
            dma((3, parts, nr)),
            dma((3, parts, nc)),
            dma((3, parts, nc)),
        ],
        compiler_params=pltpu.CompilerParams(
            collective_id=0, has_side_effects=True, vmem_limit_bytes=vmem_bytes
        ),
        cost_estimate=pl.CostEstimate(
            flops=flops, bytes_accessed=4 * blk * blk * (slots + bslots + pb), transcendentals=0
        ),
    )(f, d, a, src, tgt, cnt, b, clu, btgt, bcnt, w, lab)


def solution(mesh):
    tensor = P("row", "col", None, None, None)
    index = P("row", "col", None)
    plain = P("row", "col", None, None)
    tally = P("row", "col")
    return jax.shard_map(
        functools.partial(body, mesh.shape["row"], mesh.shape["col"]),
        mesh=mesh,
        in_specs=(tensor, tensor, tensor, index, index, tally, tensor, index, index, tally, plain, plain),
        out_specs=(tensor, tensor, P("row", None, None, None)),
        check_vma=False,
    )
```

```python
import functools

import jax
import jax.numpy as jnp
from jax import lax
from jax.experimental import pallas as pl
from jax.experimental.pallas import tpu as pltpu
from jax.sharding import PartitionSpec as P

omega = 0.7
MESH = pl.DeviceIdType.MESH
f32, bf16 = jnp.float32, jnp.bfloat16
unrolled_most = 8
slot_group = 16
vmem_bytes = 60 * 1024 * 1024
halves = 2


def loop(low, high, step):
    if high - low <= unrolled_most:
        for index in range(low, high):
            step(index)
    else:

        def one(index, carry):
            step(index)
            return carry

        lax.fori_loop(low, high, one, 0)


def split(value):
    high = value.astype(bf16)
    low = (value - high.astype(f32)).astype(bf16)
    return high, low


def wide(value):
    return jnp.concatenate(split(value), axis=-1)


def times(left, weight):
    both = jnp.dot(left, weight, preferred_element_type=f32)
    half = both.shape[-1] // 2
    return both[:, :half] + both[:, half:]


def kernel(
    nr, nc, parts,
    f_hbm, d_hbm, a_hbm, src_h, tgt_h, cnt_s, b_hbm, clu_h, btgt_h, bcnt_s, w_h, lab_h,
    x_out, r_out, c_out,
    f_v, d_v, a_v, b_v, wd, wa, wb, gath, xs, prod, part, pieces, coarse_v, onehot,
    x_v, r_v, c_v, live_a, live_b, src_s, tgt_s, clu_s, btgt_s, w_ref, lab_ref,
    in_sem, small_sem, a_sem, out_sem, rsend, rrecv, csend, crecv,
):
    pb, nrhs, blk = f_v.shape
    some = nrhs // parts
    slots, bslots = a_v.shape[0], b_v.shape[0]
    chunks = a_sem.shape[0]
    per = slots // chunks
    row, col = lax.axis_index("row"), lax.axis_index("col")

    d_in = pltpu.make_async_copy(d_hbm.at[0, 0], d_v, in_sem.at[0])
    f_in = pltpu.make_async_copy(f_hbm.at[0, 0], f_v, in_sem.at[1])
    b_in = pltpu.make_async_copy(b_hbm.at[0, 0], b_v, in_sem.at[2])
    a_in = [
        pltpu.make_async_copy(a_hbm.at[0, 0, pl.ds(c * per, per)], a_v.at[pl.ds(c * per, per)], a_sem.at[c])
        for c in range(chunks)
    ]
    small = [
        pltpu.make_async_copy(source, held, small_sem.at[i])
        for i, (source, held) in enumerate(
            ((tgt_h, tgt_s), (src_h, src_s), (btgt_h, btgt_s), (clu_h, clu_s), (w_h, w_ref), (lab_h, lab_ref))
        )
    ]
    d_in.start()
    f_in.start()

    barrier = pltpu.get_barrier_semaphore()

    def greet_row(k):
        pl.semaphore_signal(barrier, inc=1, device_id={"row": lax.rem(row + k, nr)}, device_id_type=MESH)

    def greet_col(k):
        pl.semaphore_signal(barrier, inc=1, device_id={"col": lax.rem(col + k, nc)}, device_id_type=MESH)

    loop(1, nr, greet_row)
    loop(1, nc, greet_col)
    for copy in a_in:
        copy.start()
    for copy in small:
        copy.start()
    b_in.start()

    def rows_of(h):
        return slice(h * some, (h + 1) * some)

    def row_copy(phase, h, k, owner):
        return pltpu.make_async_remote_copy(
            src_ref=gath.at[phase, h, owner],
            dst_ref=gath.at[phase, h, owner],
            send_sem=rsend.at[phase, h, k],
            recv_sem=rrecv.at[phase, h, k],
            device_id={"row": lax.rem(row + k, nr)},
            device_id_type=MESH,
        )

    def spread(phase, h):
        loop(1, nr, lambda k: row_copy(phase, h, k, row).start())

    def collect(phase, h):
        def take(owner):
            for p in range(pb):
                xs[owner * pb + p] = wide(gath[phase, h, owner, p])

        take(row)

        def arrive(k):
            owner = lax.rem(row + nr - k, nr)
            row_copy(phase, h, k, owner).wait_recv()
            take(owner)

        loop(1, nr, arrive)

    def piece_copy(phase, h, k, owner, source):
        return pltpu.make_async_remote_copy(
            src_ref=part.at[phase, h, owner],
            dst_ref=pieces.at[phase, h, source],
            send_sem=csend.at[phase, h, k],
            recv_sem=crecv.at[phase, h, k],
            device_id={"col": lax.rem(col + k, nc)},
            device_id_type=MESH,
        )

    def coarse_copy(h, k, source):
        return pltpu.make_async_remote_copy(
            src_ref=coarse_v.at[h, source],
            dst_ref=coarse_v.at[h, source],
            send_sem=csend.at[2, h, k],
            recv_sem=crecv.at[2, h, k],
            device_id={"col": lax.rem(col + k, nc)},
            device_id_type=MESH,
        )

    def source_of(k):
        return lax.rem(col + nc - k, nc)

    def prepare(weight, k, tile):
        both = wide(tile)
        weight[k, :blk] = both
        weight[k, blk:] = both

    def products(weight, target, count):
        def group(index, carry):
            for j in range(slot_group):
                s = index * slot_group + j
                prod[s] = times(xs[target[0, 0, s]], weight[s])
            return carry

        lax.fori_loop(0, count // slot_group, group, 0)

    def chosen(live, count, first):
        totals = [jnp.zeros((some, blk), f32) for p in range(pb)]
        for s in range(count):
            held, block = prod[s], live[s] - first
            totals = [total + jnp.where(block == p, held, 0.0) for p, total in enumerate(totals)]
        return totals

    def forward(phase, h):
        collect(phase, h)
        products(wa, tgt_s, slots)

        def piece(k, carry):
            owner = lax.rem(col + k, nc)
            for p, total in enumerate(chosen(live_a, slots, owner * pb)):
                part[phase, h, owner, p] = total

            @pl.when(k < nc)
            def _():
                piece_copy(phase, h, k, owner, col).start()

            return carry

        lax.fori_loop(1, nc + 1, piece, 0)

    def both(step):
        def one(h, carry):
            step(h)
            return carry

        lax.fori_loop(0, parts, one, 0)

    def image(phase, h):
        loop(1, nc, lambda k: piece_copy(phase, h, k, col, source_of(k)).wait_recv())
        totals = [part[phase, h, col, p] for p in range(pb)]
        for k in range(1, nc):
            totals = [total + pieces[phase, h, source_of(k), p] for p, total in enumerate(totals)]
        return totals

    d_in.wait()
    for p in range(pb):
        prepare(wd, p, d_v[p])
    f_in.wait()
    for p in range(pb):
        x = omega * times(wide(f_v[p]), wd[p])
        for h in range(parts):
            gath[0, h, row, p] = x[rows_of(h)]
    pl.semaphore_wait(barrier, nr + nc - 2)
    for h in range(parts):
        spread(0, h)

    for c in range(chunks):
        a_in[c].wait()

        def prepare_a(j, carry):
            for i in range(4):
                prepare(wa, c * per + 4 * j + i, a_v[c * per + 4 * j + i])
            return carry

        lax.fori_loop(0, per // 4, prepare_a, 0)

    for copy in small:
        copy.wait()

    def keep_a(s, carry):
        live_a[s] = jnp.where(s < cnt_s[0, 0], src_s[0, 0, s], -1)
        return carry

    lax.fori_loop(0, slots, keep_a, 0)

    both(lambda h: forward(0, h))

    b_in.wait()

    def prepare_b(j, carry):
        for i in range(4):
            prepare(wb, 4 * j + i, b_v[4 * j + i])
        return carry

    def keep_b(s, carry):
        live_b[s] = jnp.where(s < bcnt_s[0, 0], clu_s[0, 0, s], -1)
        return carry

    for h in range(parts):
        total = image(0, h)
        for p in range(pb):
            right = f_v[p, rows_of(h)] - total[p]
            x = gath[0, h, row, p] + omega * times(wide(right), wd[p])
            gath[1, h, row, p] = x
            x_v[p, rows_of(h)] = x
        spread(1, h)
    x_copy = pltpu.make_async_copy(x_v, x_out.at[0, 0], out_sem.at[0])
    x_copy.start()

    lax.fori_loop(0, bslots // 4, prepare_b, 0)
    lax.fori_loop(0, bslots, keep_b, 0)
    aggregate = lax.broadcasted_iota(jnp.int32, (pb * blk, blk), 0)
    for p in range(pb):
        same = aggregate == lab_ref[0, 0, p : p + 1, :]
        onehot[:, p * blk : (p + 1) * blk] = jnp.where(same, 1.0, 0.0).astype(bf16)

    both(lambda h: forward(1, h))
    for h in range(parts):
        total = image(1, h)
        for p in range(pb):
            left = f_v[p, rows_of(h)] - total[p]
            gath[2, h, row, p] = left
            r_v[p, rows_of(h)] = left
        spread(2, h)
    r_copy = pltpu.make_async_copy(r_v, r_out.at[0, 0], out_sem.at[1])
    r_copy.start()

    weighted = jnp.concatenate([r_v[p] * w_ref[0, 0, p : p + 1, :] for p in range(pb)], axis=-1)
    contract = functools.partial(
        lax.dot_general,
        dimension_numbers=(((1,), (1,)), ((), ())),
        preferred_element_type=f32,
    )
    high, low = split(weighted)
    tentative = contract(high, onehot[...]) + contract(low, onehot[...])
    for p in range(pb):
        for h in range(parts):
            coarse_v[h, col, p] = tentative[rows_of(h), p * blk : (p + 1) * blk]

    def restrict(h):
        collect(2, h)
        products(wb, btgt_s, bslots)
        for p, total in enumerate(chosen(live_b, bslots, 0)):
            coarse_v[h, col, p] = coarse_v[h, col, p] + total
        loop(1, nc, lambda k: coarse_copy(h, k, col).start())

    both(restrict)

    for phase in range(3):
        for h in range(parts):
            loop(1, nr, lambda k: row_copy(phase, h, k, row).wait_send())
    for phase in range(2):
        for h in range(parts):
            loop(1, nc, lambda k: piece_copy(phase, h, k, lax.rem(col + k, nc), col).wait_send())
    x_copy.wait()
    r_copy.wait()
    for h in range(parts):
        loop(1, nc, lambda k: coarse_copy(h, k, source_of(k)).wait_recv())
        for p in range(pb):
            c_v[p, rows_of(h)] = jnp.sum(coarse_v[h, :, p], axis=0)
    c_copy = pltpu.make_async_copy(c_v, c_out.at[0], out_sem.at[2])
    c_copy.start()
    for h in range(parts):
        loop(1, nc, lambda k: coarse_copy(h, k, col).wait_send())
    c_copy.wait()


def body(nr, nc, *args):
    f, d, a, src, tgt, cnt, b, clu, btgt, bcnt, w, lab = args
    pb, nrhs, blk = f.shape[2:]
    slots, bslots = a.shape[2], b.shape[2]
    chunks = 4
    parts = halves
    some = (pb, nrhs // parts, blk)
    anyspace = pl.BlockSpec(memory_space=pl.ANY)
    smem = pl.BlockSpec(memory_space=pltpu.SMEM)
    block = (pb, nrhs, blk)
    dma = pltpu.SemaphoreType.DMA
    flops = 8 * (2 * slots + bslots + 3 * pb) * nrhs * blk * blk
    shapes = (
        jax.ShapeDtypeStruct(f.shape, f32),
        jax.ShapeDtypeStruct(f.shape, f32),
        jax.ShapeDtypeStruct((1,) + block, f32),
    )
    return pl.pallas_call(
        functools.partial(kernel, nr, nc, parts),
        out_shape=tuple(pltpu.VMEM(x.shape, x.dtype) for x in shapes),
        in_specs=[anyspace] * 5 + [smem] + [anyspace] * 3 + [smem] + [anyspace] * 2,
        out_specs=(anyspace,) * 3,
        scratch_shapes=[
            pltpu.VMEM(block, f32),
            pltpu.VMEM((pb, blk, blk), f32),
            pltpu.VMEM((slots, blk, blk), f32),
            pltpu.VMEM((bslots, blk, blk), f32),
            pltpu.VMEM((pb, 2 * blk, 2 * blk), bf16),
            pltpu.VMEM((slots, 2 * blk, 2 * blk), bf16),
            pltpu.VMEM((bslots, 2 * blk, 2 * blk), bf16),
            pltpu.VMEM((3, parts, nr) + some, f32),
            pltpu.VMEM((nr * pb, some[1], 2 * blk), bf16),
            pltpu.VMEM((slots, some[1], blk), f32),
            pltpu.VMEM((2, parts, nc) + some, f32),
            pltpu.VMEM((2, parts, nc) + some, f32),
            pltpu.VMEM((parts, nc) + some, f32),
            pltpu.VMEM((pb * blk, pb * blk), bf16),
            pltpu.VMEM(block, f32),
            pltpu.VMEM(block, f32),
            pltpu.VMEM(block, f32),
            pltpu.SMEM((slots,), jnp.int32),
            pltpu.SMEM((bslots,), jnp.int32),
            pltpu.SMEM(src.shape, jnp.int32),
            pltpu.SMEM(tgt.shape, jnp.int32),
            pltpu.SMEM(clu.shape, jnp.int32),
            pltpu.SMEM(btgt.shape, jnp.int32),
            pltpu.VMEM(w.shape, f32),
            pltpu.VMEM(lab.shape, jnp.int32),
            dma((3,)),
            dma((6,)),
            dma((chunks,)),
            dma((3,)),
            dma((3, parts, nr)),
            dma((3, parts, nr)),
            dma((3, parts, nc)),
            dma((3, parts, nc)),
        ],
        compiler_params=pltpu.CompilerParams(
            collective_id=0, has_side_effects=True, vmem_limit_bytes=vmem_bytes
        ),
        cost_estimate=pl.CostEstimate(
            flops=flops, bytes_accessed=4 * blk * blk * (slots + bslots + pb), transcendentals=0
        ),
    )(f, d, a, src, tgt, cnt, b, clu, btgt, bcnt, w, lab)


def solution(mesh):
    tensor = P("row", "col", None, None, None)
    index = P("row", "col", None)
    plain = P("row", "col", None, None)
    tally = P("row", "col")
    return jax.shard_map(
        functools.partial(body, mesh.shape["row"], mesh.shape["col"]),
        mesh=mesh,
        in_specs=(tensor, tensor, tensor, index, index, tally, tensor, index, index, tally, plain, plain),
        out_specs=(tensor, tensor, P("row", None, None, None)),
        check_vma=False,
    )
```
